32 devices in a mesh: lang: 4 (over y, core), pair: 8 (over z, x).
Axes of the slice: x: 2, y: 2, z: 4, core: 2. Of those that a mesh axis runs over, the one named last changes fastest.
Arguments:
- sentences: bfloat16 [128, 128, 1024], P(('lang', 'pair')), may hold values from -16 to 16
- cotangent: bfloat16 [128, 128, 1024], P(('lang', 'pair')), may hold values from -6 to 6
- w_query: bfloat16 [1024, 1024], replicated, may hold values from -0.1875 to 0.1875
- w_key: bfloat16 [1024, 1024], replicated, may hold values from -0.1875 to 0.1875
- w_value: bfloat16 [1024, 1024], replicated, may hold values from -0.1875 to 0.1875
- send_rows: int32 [32, 4, 1], P(('lang', 'pair')), may hold values from 0 to 3
- pair_src: int32 [32, 16], P(('lang', 'pair')), may hold values from 0 to 3
- pair_slot: int32 [32, 16], P(('lang', 'pair')), may hold values from 0 to 3
- pair_valid: int32 [32, 16], P(('lang', 'pair')), may hold values 0 or 1
Outputs:
- attended: bfloat16 [128, 128, 1024], P(('lang', 'pair'))
- grad_sentences: bfloat16 [128, 128, 1024], P(('lang', 'pair'))
- grad_wq: bfloat16 [1024, 1024], replicated
- grad_wk: bfloat16 [1024, 1024], replicated
- grad_wv: bfloat16 [1024, 1024], replicated
The draws below stay inside these ranges and needn't reach their ends.
All inputs are finite; a program needn't handle non-finite values. No bound on the sum of `pair_valid` on one device may be relied on, other than what follows from the above.
Results may differ from the reference program's by a relative error of at most 0.015.
The reference program's roundings to bfloat16 on the way (of `prob_b` and `dscore`) count: a program that leaves them out, or rounds other values in their place, can miss the bound.
Values may be sent and summed in bfloat16 or wider, within the bound.
A program may use at most 128 MiB of HBM per device.

```python
import jax
import jax.numpy as jnp
from jax import lax

D = 1024
HEADS = 16
L = 128
SENT_DEV = 4
PAIRS_DEV = 16
CAP = 1
SENTENCES = 128
N_LANG = 4
DEVICES = 32


def draw_sentences(key, part):
    key = jax.random.fold_in(key, 7)
    base = jax.random.normal(key, (SENTENCES, L, D), jnp.float32)
    base = jnp.clip(base, -6.0, 6.0)
    return base.astype(jnp.bfloat16)


def with_ends(result, own_key, smallest, largest):
    spot = [jax.random.randint(jax.random.fold_in(own_key, axis), (), 0, length) for axis, length in enumerate(result.shape)]
    widest = result.shape.index(max(result.shape))
    beside = spot[:widest] + [(spot[widest] + 1) % result.shape[widest]] + spot[widest + 1:]
    return result.at[tuple(spot)].set(smallest).at[tuple(beside)].set(largest)


def block_scale(rng, dims, pieces, least, high):
    factor_of = 1.0
    for axis_at, blocks in pieces:
        heights = jax.random.uniform(jax.random.fold_in(jax.random.fold_in(rng, 6), axis_at), (blocks,), jnp.float32, least / len(pieces), high / len(pieces))
        factor_of = factor_of * jnp.repeat(jnp.exp(heights), dims[axis_at] // blocks).reshape((-1,) + (1,) * (len(dims) - 1 - axis_at))
    return factor_of


def noise(own_key, extent, scale, reach, cuts=(), held_as=jnp.bfloat16):
    level = block_scale(own_key, extent, cuts, -0.22, 0.18) if cuts else 1.0
    drawn = jax.random.normal(own_key, extent, jnp.float32) * scale * level
    return jnp.minimum(jnp.maximum(drawn, -reach), reach).astype(held_as)


def setup_inputs(seed: int = 0) -> dict:
    streams_of = jax.random.split(jax.random.key(seed), 10)
    return {
        "sentences": draw_sentences(jax.random.fold_in(streams_of[9], 71), 0),
        "cotangent": noise(streams_of[1], (SENTENCES, L, D), 1.0, 6.0, ((0, 32),)),
        "w_query": noise(streams_of[2], (D, D), D ** -0.5, 0.1875),
        "w_key": noise(streams_of[3], (D, D), D ** -0.5, 0.1875),
        "w_value": noise(streams_of[4], (D, D), D ** -0.5, 0.1875),
        "send_rows": with_ends(jax.random.randint(streams_of[5], (DEVICES, N_LANG, CAP), 0, SENT_DEV), jax.random.fold_in(streams_of[5], 1), 0, SENT_DEV - 1).astype(jnp.int32),
        "pair_src": with_ends(jax.random.randint(streams_of[6], (DEVICES, PAIRS_DEV), 0, SENT_DEV), jax.random.fold_in(streams_of[6], 1), 0, SENT_DEV - 1).astype(jnp.int32),
        "pair_slot": with_ends(jax.random.randint(streams_of[7], (DEVICES, PAIRS_DEV), 0, N_LANG * CAP), jax.random.fold_in(streams_of[7], 1), 0, (N_LANG * CAP) - 1).astype(jnp.int32),
        "pair_valid": with_ends((jax.random.randint(streams_of[8], (DEVICES, PAIRS_DEV), 0, 4) < 3).astype(jnp.int32), jax.random.fold_in(streams_of[8], 1), 0, 1),
    }


def attend_block(q_rows, k_rows, v_rows, g_rows, valid, heads):
    count, length, width = q_rows.shape
    size = width // heads
    scale = size ** -0.5
    qh = q_rows.reshape(count, length, heads, size).astype(jnp.float32)
    kh = k_rows.reshape(count, length, heads, size).astype(jnp.float32)
    vh = v_rows.reshape(count, length, heads, size).astype(jnp.float32)
    mult = valid.astype(jnp.float32)[:, None, None, None]
    gh = g_rows.reshape(count, length, heads, size).astype(jnp.float32) * mult
    scores = jnp.einsum('bqhd,bkhd->bhqk', qh, kh) * scale
    scores = scores - jnp.max(scores, axis=-1, keepdims=True)
    prob = jnp.exp(scores)
    prob = prob / jnp.sum(prob, axis=-1, keepdims=True)
    prob_b = prob.astype(jnp.bfloat16).astype(jnp.float32)
    outp = jnp.einsum('bhqk,bkhd->bqhd', prob_b, vh) * mult
    dvalue = jnp.einsum('bhqk,bqhd->bkhd', prob_b, gh)
    dprob = jnp.einsum('bqhd,bkhd->bhqk', gh, vh)
    dscore = prob * (dprob - jnp.sum(prob * dprob, axis=-1, keepdims=True)) * scale
    dscore = dscore.astype(jnp.bfloat16).astype(jnp.float32)
    dquery = jnp.einsum('bhqk,bkhd->bqhd', dscore, kh)
    dkey = jnp.einsum('bhqk,bqhd->bkhd', dscore, qh)
    shape = (count, length, width)
    return outp.reshape(shape), dquery.reshape(shape), dkey.reshape(shape), dvalue.reshape(shape)


def reference(sentences, cotangent, w_query, w_key, w_value, send_rows, pair_src, pair_slot, pair_valid):
    n_lang = send_rows.shape[1]
    n_dev = send_rows.shape[0]
    n_pair = n_dev // n_lang
    flat = sentences.reshape(-1, D)
    queries = jnp.dot(flat, w_query, preferred_element_type=jnp.float32).astype(jnp.bfloat16).reshape(SENTENCES, L, D)
    keys = jnp.dot(flat, w_key, preferred_element_type=jnp.float32).astype(jnp.bfloat16).reshape(SENTENCES, L, D)
    values = jnp.dot(flat, w_value, preferred_element_type=jnp.float32).astype(jnp.bfloat16).reshape(SENTENCES, L, D)
    dev_ids = jnp.arange(n_dev, dtype=jnp.int32)
    group = dev_ids // n_pair
    place = dev_ids % n_pair
    slot_ids = jnp.arange(n_lang * CAP, dtype=jnp.int32)
    sender = (slot_ids // CAP)[None, :] * n_pair + place[:, None]
    entry = send_rows[sender, group[:, None], (slot_ids % CAP)[None, :]]
    targets = (sender * SENT_DEV + entry).astype(jnp.int32)
    block = 4
    slots = n_lang * CAP

    def one_device(carry, dev):
        grad_t, gwq, gwk, gwv = carry
        local_src = pair_src[dev]
        src_g = dev * SENT_DEV + local_src
        tgt_slots = targets[dev]
        pslot = pair_slot[dev]
        valid = pair_valid[dev]
        zeros_s = jnp.zeros((SENT_DEV, L, D), jnp.float32)
        zeros_t = jnp.zeros((slots, L, D), jnp.float32)

        def step(i, acc):
            out_acc, dq_acc, dk_acc, dv_acc = acc
            lo = i * block
            srcs = lax.dynamic_slice_in_dim(src_g, lo, block)
            locs = lax.dynamic_slice_in_dim(local_src, lo, block)
            sl = lax.dynamic_slice_in_dim(pslot, lo, block)
            vl = lax.dynamic_slice_in_dim(valid, lo, block)
            tg = tgt_slots[sl]
            outp, dquery, dkey, dvalue = attend_block(queries[srcs], keys[tg], values[tg], cotangent[srcs], vl, HEADS)
            return (out_acc.at[locs].add(outp), dq_acc.at[locs].add(dquery), dk_acc.at[sl].add(dkey), dv_acc.at[sl].add(dvalue))

        out_acc, dq_acc, dk_acc, dv_acc = lax.fori_loop(0, PAIRS_DEV // block, step, (zeros_s, zeros_s, zeros_t, zeros_t))
        dq_b = dq_acc.astype(jnp.bfloat16).reshape(-1, D)
        dk_b = dk_acc.astype(jnp.bfloat16).reshape(-1, D)
        dv_b = dv_acc.astype(jnp.bfloat16).reshape(-1, D)
        own = lax.dynamic_slice_in_dim(sentences, dev * SENT_DEV, SENT_DEV).reshape(-1, D)
        grad_src = jnp.dot(dq_b, w_query.T, preferred_element_type=jnp.float32)
        rows_t = sentences[tgt_slots].reshape(-1, D)
        dxt = jnp.dot(dk_b, w_key.T, preferred_element_type=jnp.float32) + jnp.dot(dv_b, w_value.T, preferred_element_type=jnp.float32)
        grad_t = grad_t.at[tgt_slots].add(dxt.reshape(slots, L, D))
        gwq = gwq + jnp.dot(own.T, dq_b, preferred_element_type=jnp.float32)
        gwk = gwk + jnp.dot(rows_t.T, dk_b, preferred_element_type=jnp.float32)
        gwv = gwv + jnp.dot(rows_t.T, dv_b, preferred_element_type=jnp.float32)
        return (grad_t, gwq, gwk, gwv), (out_acc.astype(jnp.bfloat16), grad_src.reshape(SENT_DEV, L, D))

    square = jnp.zeros((D, D), jnp.float32)
    start = (jnp.zeros((SENTENCES, L, D), jnp.float32), square, square, square)
    (grad_t, gwq, gwk, gwv), (attended, grad_src) = lax.scan(one_device, start, dev_ids)
    attended = attended.reshape(SENTENCES, L, D)
    grad_sentences = (grad_src.reshape(SENTENCES, L, D) + grad_t).astype(jnp.bfloat16)
    factor = 1.0 / (SENTENCES * L) ** 0.5
    return attended, grad_sentences, (gwq * factor).astype(jnp.bfloat16), (gwk * factor).astype(jnp.bfloat16), (gwv * factor).astype(jnp.bfloat16)
```

```python
import jax
import jax.numpy as jnp
from jax import lax
from jax.experimental import pallas as pl
from jax.experimental.pallas import tpu as pltpu
from jax.sharding import PartitionSpec as P

HEADS = 16
LANES = 128
GROUP = 256


def attend_kernel(
    src_ref, slot_ref, valid_ref, q_ref, k_ref, v_ref, g_ref,
    out_ref, dq_ref, dk_ref, dv_ref,
    bd, kv, kvt, out_t, dq_t, dkv, counts,
):
    n_src, length, width = q_ref.shape
    n_slot = k_ref.shape[0]
    size = LANES // 2
    scale = size ** (-0.5)
    blocks = width // LANES
    n_pairs = src_ref.shape[0]
    low = lax.broadcasted_iota(jnp.int32, (length, LANES), 1) < size

    def clear(i, _):
        counts[i] = 0
        return 0

    lax.fori_loop(0, n_src * n_slot, clear, 0)

    def count(j, _):
        key = src_ref[j] * n_slot + slot_ref[j]
        counts[key] = counts[key] + valid_ref[j]
        return 0

    lax.fori_loop(0, n_pairs, count, 0)

    def set_source(s, _):
        for b in range(blocks):
            cols = slice(b * LANES, (b + 1) * LANES)
            q = q_ref[s, :, cols].astype(jnp.float32) * scale
            g = pltpu.roll(g_ref[s, :, cols].astype(jnp.float32), size, 1)
            bd[s, 2 * b, :length] = jnp.where(low, q, 0.0).astype(jnp.bfloat16)
            bd[s, 2 * b, length:] = jnp.where(low, 0.0, g).astype(jnp.bfloat16)
            bd[s, 2 * b + 1, :length] = jnp.where(low, 0.0, q).astype(jnp.bfloat16)
            bd[s, 2 * b + 1, length:] = jnp.where(low, g, 0.0).astype(jnp.bfloat16)
        out_t[s] = jnp.zeros((width, length), jnp.float32)
        dq_t[s] = jnp.zeros((width, length), jnp.float32)
        return 0

    lax.fori_loop(0, n_src, set_source, 0)

    def set_slot(t, _):
        for b in range(blocks):
            cols = slice(b * LANES, (b + 1) * LANES)
            k = k_ref[t, :, cols].astype(jnp.float32)
            v = pltpu.roll(v_ref[t, :, cols].astype(jnp.float32), size, 1)
            even = jnp.where(low, k, v)
            odd = jnp.where(low, v, k)
            kv[t, 2 * b] = even.astype(jnp.bfloat16)
            kv[t, 2 * b + 1] = odd.astype(jnp.bfloat16)
            kvt[t, 2 * b] = even.T.astype(jnp.bfloat16)
            kvt[t, 2 * b + 1] = odd.T.astype(jnp.bfloat16)
            dkv[t, 2 * b] = jnp.zeros((length, LANES), jnp.float32)
            dkv[t, 2 * b + 1] = jnp.zeros((length, LANES), jnp.float32)
        return 0

    lax.fori_loop(0, n_slot, set_slot, 0)

    def combo(i, _):
        times = counts[i]

        @pl.when(times > 0)
        def _():
            s = i // n_slot
            t = i - s * n_slot
            w = times.astype(jnp.float32)
            both = []
            for h in range(2 * blocks):
                both.append(lax.dot_general(
                    kv[t, h], bd[s, h], (((1,), (1,)), ((), ())),
                    preferred_element_type=jnp.float32))
            mixed = []
            for h in range(2 * blocks):
                sc = both[h][:, :length]
                dp = both[h][:, length:]
                e = jnp.exp(sc - jnp.max(sc, axis=0, keepdims=True))
                p = e * (1.0 / jnp.sum(e, axis=0, keepdims=True))
                ds = p * (dp - jnp.sum(p * dp, axis=0, keepdims=True))
                mixed.append(jnp.concatenate(
                    [ds.astype(jnp.bfloat16), p.astype(jnp.bfloat16)], axis=1))
            for h in range(2 * blocks):
                x = mixed[h]
                dkv[t, h] += w * jnp.dot(x, bd[s, h], preferred_element_type=jnp.float32)
                r = jnp.dot(kvt[t, h], x, preferred_element_type=jnp.float32)
                rows = slice(h * size, (h + 1) * size)
                first, second = slice(0, size), slice(size, 2 * size)
                key_rows, value_rows = (first, second) if h % 2 == 0 else (second, first)
                dq_t[s, rows] += w * r[key_rows, :length]
                out_t[s, rows] += w * r[value_rows, length:]

        return 0

    lax.fori_loop(0, n_src * n_slot, combo, 0)

    def put_source(s, _):
        for b in range(blocks):
            cols = slice(b * LANES, (b + 1) * LANES)
            out_ref[s, :, cols] = out_t[s, cols].T.astype(jnp.bfloat16)
            dq_ref[s, :, cols] = (dq_t[s, cols].T * scale).astype(jnp.bfloat16)
        return 0

    lax.fori_loop(0, n_src, put_source, 0)

    def put_slot(t, _):
        for b in range(blocks):
            cols = slice(b * LANES, (b + 1) * LANES)
            even, odd = dkv[t, 2 * b], dkv[t, 2 * b + 1]
            dk_ref[t, :, cols] = jnp.where(low, even, odd).astype(jnp.bfloat16)
            dv_ref[t, :, cols] = pltpu.roll(jnp.where(low, odd, even), size, 1).astype(jnp.bfloat16)
        return 0

    lax.fori_loop(0, n_slot, put_slot, 0)


def attend(group, src, slot, valid, queries, keys, values, cotangent):
    n_src, length, _ = queries.shape
    n_slot = keys.shape[0]
    heads = GROUP // 64
    smem = pl.BlockSpec(memory_space=pltpu.SMEM)

    def cut(rows):
        return pl.BlockSpec((rows, length, GROUP), lambda i: (0, 0, group))

    def whole(rows):
        return pl.BlockSpec((rows, length, GROUP), lambda i: (0, 0, 0))

    def made(rows):
        return jax.ShapeDtypeStruct((rows, length, GROUP), jnp.bfloat16)

    return pl.pallas_call(
        attend_kernel,
        grid=(1,),
        in_specs=[smem, smem, smem, cut(n_src), cut(n_slot), cut(n_slot), cut(n_src)],
        out_specs=[whole(n_src), whole(n_src), whole(n_slot), whole(n_slot)],
        out_shape=[made(n_src), made(n_src), made(n_slot), made(n_slot)],
        scratch_shapes=[
            pltpu.VMEM((n_src, heads, 2 * length, LANES), jnp.bfloat16),
            pltpu.VMEM((n_slot, heads, length, LANES), jnp.bfloat16),
            pltpu.VMEM((n_slot, heads, LANES, length), jnp.bfloat16),
            pltpu.VMEM((n_src, GROUP, length), jnp.float32),
            pltpu.VMEM((n_src, GROUP, length), jnp.float32),
            pltpu.VMEM((n_slot, heads, length, LANES), jnp.float32),
            pltpu.SMEM((n_src * n_slot,), jnp.int32),
        ],
        compiler_params=pltpu.CompilerParams(vmem_limit_bytes=32 * 1024 * 1024),
        cost_estimate=pl.CostEstimate(
            flops=3000000000, bytes_accessed=30000000, transcendentals=1000000),
    )(src, slot, valid, queries, keys, values, cotangent)


def project(rows, weight):
    return (
        jnp.dot(rows.reshape(-1, rows.shape[-1]), weight, preferred_element_type=jnp.float32)
        .astype(jnp.bfloat16)
        .reshape(rows.shape)
    )


def body(sentences, cotangent, w_query, w_key, w_value, send_rows, pair_src, pair_slot, pair_valid):
    sent_dev, length, width = sentences.shape
    n_lang = lax.axis_size("lang")
    n_pair = lax.axis_size("pair")
    cap = send_rows.shape[2]
    slots = n_lang * cap
    axes = ("lang", "pair")
    listed = send_rows[0].reshape(-1)
    outgoing = jnp.take(sentences, listed, axis=0).reshape(n_lang, cap, length, width)
    received = lax.all_to_all(outgoing, "lang", split_axis=0, concat_axis=0, tiled=True).reshape(
        slots, length, width
    )
    queries = project(sentences, w_query)
    keys = project(received, w_key)
    values = project(received, w_value)
    own_flat = sentences.reshape(-1, width)
    recv_flat = received.reshape(-1, width)
    contract = (((0,), (0,)), ((), ()))
    parts, sums = [], []
    for group in range(width // GROUP):
        out, dq, dk, dv = attend(
            group, pair_src[0], pair_slot[0], pair_valid[0], queries, keys, values, cotangent)
        parts.append((out, dq, dk, dv))
        gwq = lax.dot_general(own_flat, dq.reshape(-1, GROUP), contract,
                              preferred_element_type=jnp.float32)
        gwk = lax.dot_general(recv_flat, dk.reshape(-1, GROUP), contract,
                              preferred_element_type=jnp.float32)
        gwv = lax.dot_general(recv_flat, dv.reshape(-1, GROUP), contract,
                              preferred_element_type=jnp.float32)
        sums.append(lax.psum_scatter(
            jnp.concatenate([gwq, gwk, gwv], axis=1), axes, scatter_dimension=0, tiled=True))
    attended, dq_b, dk_b, dv_b = (
        jnp.concatenate([part[i] for part in parts], axis=2) for i in range(4))
    flat = (-1, width)
    dxt = jnp.dot(dk_b.reshape(flat), w_key.T, preferred_element_type=jnp.float32) + jnp.dot(
        dv_b.reshape(flat), w_value.T, preferred_element_type=jnp.float32
    )
    returned = lax.all_to_all(
        dxt.reshape(n_lang, cap, length, width), "lang", split_axis=0, concat_axis=0, tiled=True
    )
    grad_src = jnp.dot(dq_b.reshape(flat), w_query.T, preferred_element_type=jnp.float32).reshape(
        sent_dev, length, width
    )
    pick = (listed[None, :] == jnp.arange(sent_dev, dtype=listed.dtype)[:, None])
    returned = returned.reshape(slots, length, width)
    grad_total = grad_src
    for t in range(slots):
        grad_total = grad_total + jnp.where(pick[:, t, None, None], returned[t][None], 0.0)
    factor = 1.0 / (sent_dev * n_lang * n_pair * length) ** 0.5
    grads = []
    for i in range(3):
        mine = jnp.concatenate([total[:, i * GROUP:(i + 1) * GROUP] for total in sums], axis=1)
        grads.append(lax.all_gather(
            (mine * factor).astype(jnp.bfloat16), axes, axis=0, tiled=True))
    return (attended, grad_total.astype(jnp.bfloat16), *grads)


def solution(mesh):
    in_specs = (
        P(("lang", "pair"), None, None),
        P(("lang", "pair"), None, None),
        P(),
        P(),
        P(),
        P(("lang", "pair"), None, None),
        P(("lang", "pair"), None),
        P(("lang", "pair"), None),
        P(("lang", "pair"), None),
    )
    out_specs = (P(("lang", "pair"), None, None), P(("lang", "pair"), None, None), P(), P(), P())
    return jax.shard_map(body, mesh=mesh, in_specs=in_specs, out_specs=out_specs, check_vma=False)
```

```python
import jax
import jax.numpy as jnp
from jax import lax
from jax.experimental import pallas as pl
from jax.experimental.pallas import tpu as pltpu
from jax.sharding import PartitionSpec as P

HEADS = 16
LANES = 128
GROUP = 256


def attend_kernel(
    src_ref, slot_ref, valid_ref, q_ref, k_ref, v_ref, g_ref,
    out_ref, dq_ref, dk_ref, dv_ref,
    bd, kv, kvt, out_t, dq_t, dkv, counts,
):
    n_src, length, width = q_ref.shape
    n_slot = k_ref.shape[0]
    size = LANES // 2
    scale = size ** (-0.5)
    blocks = width // LANES
    n_pairs = src_ref.shape[0]
    low = lax.broadcasted_iota(jnp.int32, (length, LANES), 1) < size

    def clear(i, _):
        counts[i] = 0
        return 0

    lax.fori_loop(0, n_src * n_slot, clear, 0)

    def count(j, _):
        key = src_ref[j] * n_slot + slot_ref[j]
        counts[key] = counts[key] + valid_ref[j]
        return 0

    lax.fori_loop(0, n_pairs, count, 0)

    def set_source(s, _):
        for b in range(blocks):
            cols = slice(b * LANES, (b + 1) * LANES)
            q = q_ref[s, :, cols].astype(jnp.float32) * scale
            g = pltpu.roll(g_ref[s, :, cols].astype(jnp.float32), size, 1)
            bd[s, 2 * b, :length] = jnp.where(low, q, 0.0).astype(jnp.bfloat16)
            bd[s, 2 * b, length:] = jnp.where(low, 0.0, g).astype(jnp.bfloat16)
            bd[s, 2 * b + 1, :length] = jnp.where(low, 0.0, q).astype(jnp.bfloat16)
            bd[s, 2 * b + 1, length:] = jnp.where(low, g, 0.0).astype(jnp.bfloat16)
        out_t[s] = jnp.zeros((width, length), jnp.float32)
        dq_t[s] = jnp.zeros((width, length), jnp.float32)
        return 0

    lax.fori_loop(0, n_src, set_source, 0)

    def set_slot(t, _):
        for b in range(blocks):
            cols = slice(b * LANES, (b + 1) * LANES)
            k = k_ref[t, :, cols].astype(jnp.float32)
            v = pltpu.roll(v_ref[t, :, cols].astype(jnp.float32), size, 1)
            even = jnp.where(low, k, v)
            odd = jnp.where(low, v, k)
            kv[t, 2 * b] = even.astype(jnp.bfloat16)
            kv[t, 2 * b + 1] = odd.astype(jnp.bfloat16)
            kvt[t, 2 * b] = even.T.astype(jnp.bfloat16)
            kvt[t, 2 * b + 1] = odd.T.astype(jnp.bfloat16)
            dkv[t, 2 * b] = jnp.zeros((length, LANES), jnp.float32)
            dkv[t, 2 * b + 1] = jnp.zeros((length, LANES), jnp.float32)
        return 0

    lax.fori_loop(0, n_slot, set_slot, 0)

    def combo(i, _):
        times = counts[i]

        @pl.when(times > 0)
        def _():
            s = i // n_slot
            t = i - s * n_slot
            w = times.astype(jnp.float32)
            both = []
            for h in range(2 * blocks):
                both.append(lax.dot_general(
                    kv[t, h], bd[s, h], (((1,), (1,)), ((), ())),
                    preferred_element_type=jnp.float32))
            mixed = []
            for h in range(2 * blocks):
                sc = both[h][:, :length]
                dp = both[h][:, length:]
                e = jnp.exp(sc - jnp.max(sc, axis=0, keepdims=True))
                p = e * (1.0 / jnp.sum(e, axis=0, keepdims=True))
                ds = p * (dp - jnp.sum(p * dp, axis=0, keepdims=True))
                mixed.append(jnp.concatenate(
                    [ds.astype(jnp.bfloat16), p.astype(jnp.bfloat16)], axis=1))
            for h in range(2 * blocks):
                x = mixed[h]
                dkv[t, h] += w * jnp.dot(x, bd[s, h], preferred_element_type=jnp.float32)
                r = jnp.dot(kvt[t, h], x, preferred_element_type=jnp.float32)
                rows = slice(h * size, (h + 1) * size)
                first, second = slice(0, size), slice(size, 2 * size)
                key_rows, value_rows = (first, second) if h % 2 == 0 else (second, first)
                dq_t[s, rows] += w * r[key_rows, :length]
                out_t[s, rows] += w * r[value_rows, length:]

        return 0

    lax.fori_loop(0, n_src * n_slot, combo, 0)

    def put_source(s, _):
        for b in range(blocks):
            cols = slice(b * LANES, (b + 1) * LANES)
            out_ref[s, :, cols] = out_t[s, cols].T.astype(jnp.bfloat16)
            dq_ref[s, :, cols] = (dq_t[s, cols].T * scale).astype(jnp.bfloat16)
        return 0

    lax.fori_loop(0, n_src, put_source, 0)

    def put_slot(t, _):
        for b in range(blocks):
            cols = slice(b * LANES, (b + 1) * LANES)
            even, odd = dkv[t, 2 * b], dkv[t, 2 * b + 1]
            dk_ref[t, :, cols] = jnp.where(low, even, odd).astype(jnp.bfloat16)
            dv_ref[t, :, cols] = pltpu.roll(jnp.where(low, odd, even), size, 1).astype(jnp.bfloat16)
        return 0

    lax.fori_loop(0, n_slot, put_slot, 0)


def attend(src, slot, valid, queries, keys, values, cotangent):
    n_src, length, width = queries.shape
    n_slot = keys.shape[0]
    heads = 2 * GROUP // LANES
    smem = pl.BlockSpec(memory_space=pltpu.SMEM)

    def cut(rows):
        return pl.BlockSpec((rows, length, GROUP), lambda i: (0, 0, i))

    def made(rows):
        return jax.ShapeDtypeStruct((rows, length, width), jnp.bfloat16)

    return pl.pallas_call(
        attend_kernel,
        grid=(width // GROUP,),
        in_specs=[smem, smem, smem, cut(n_src), cut(n_slot), cut(n_slot), cut(n_src)],
        out_specs=[cut(n_src), cut(n_src), cut(n_slot), cut(n_slot)],
        out_shape=[made(n_src), made(n_src), made(n_slot), made(n_slot)],
        scratch_shapes=[
            pltpu.VMEM((n_src, heads, 2 * length, LANES), jnp.bfloat16),
            pltpu.VMEM((n_slot, heads, length, LANES), jnp.bfloat16),
            pltpu.VMEM((n_slot, heads, LANES, length), jnp.bfloat16),
            pltpu.VMEM((n_src, GROUP, length), jnp.float32),
            pltpu.VMEM((n_src, GROUP, length), jnp.float32),
            pltpu.VMEM((n_slot, heads, length, LANES), jnp.float32),
            pltpu.SMEM((n_src * n_slot,), jnp.int32),
        ],
        compiler_params=pltpu.CompilerParams(vmem_limit_bytes=32 * 1024 * 1024),
        cost_estimate=pl.CostEstimate(
            flops=12000000000, bytes_accessed=30000000, transcendentals=4000000),
    )(src, slot, valid, queries, keys, values, cotangent)


def project(rows, weight):
    return (
        jnp.dot(rows.reshape(-1, rows.shape[-1]), weight, preferred_element_type=jnp.float32)
        .astype(jnp.bfloat16)
        .reshape(rows.shape)
    )


AXES = ("lang", "pair")


def swap(x, bit):
    n = lax.axis_size("lang") * lax.axis_size("pair")
    return lax.ppermute(x, AXES, [(i, i ^ (1 << bit)) for i in range(n)])


def half(x, which, axis=0):
    rows = x.shape[axis] // 2
    return lax.dynamic_slice_in_dim(x, which * rows, rows, axis)


def body(sentences, cotangent, w_query, w_key, w_value, send_rows, pair_src, pair_slot, pair_valid):
    sent_dev, length, width = sentences.shape
    n_lang = lax.axis_size("lang")
    n_pair = lax.axis_size("pair")
    cap = send_rows.shape[2]
    slots = n_lang * cap
    lang = lax.axis_index("lang")
    me = lang * n_pair + lax.axis_index("pair")
    pair_bits = n_pair.bit_length() - 1
    lang_bits = n_lang.bit_length() - 1
    core = pair_bits
    low = list(range(pair_bits // 2))
    high = list(range(pair_bits // 2, pair_bits))
    upper = list(range(pair_bits + 1, pair_bits + lang_bits))

    def exchange(x, d):
        return lax.ppermute(x, "lang", [(i, i ^ d) for i in range(n_lang)])

    listed = [lax.dynamic_index_in_dim(send_rows[0], lang ^ d, 0, False) for d in range(n_lang)]
    received = []
    for d in range(n_lang):
        block = jnp.take(sentences, listed[d], axis=0)
        received.append(exchange(block, d) if d else block)
    received = jnp.concatenate(received, axis=0)
    slot = pair_slot[0]
    slot = ((slot // cap) ^ lang) * cap + slot % cap

    queries = project(sentences, w_query)
    keys = project(received, w_key)
    values = project(received, w_value)
    attended, dq, dk, dv = attend(
        pair_src[0], slot, pair_valid[0], queries, keys, values, cotangent)
    flat = (-1, width)
    dq_b, dk_b, dv_b = dq.reshape(flat), dk.reshape(flat), dv.reshape(flat)

    my = {b: (me >> b) & 1 for b in range(pair_bits + lang_bits)}
    own_flat = sentences.reshape(flat)
    recv_flat = received.reshape(flat)
    contract = (((0,), (0,)), ((), ()))

    def outer(rows, d):
        return lax.dot_general(rows, d, contract, preferred_element_type=jnp.float32)

    jobs = [
        (recv_flat, dv_b, high + low + upper),
        (recv_flat, dk_b, upper + high + low),
        (own_flat, dq_b, low + upper + high),
    ]
    got = [swap(outer(half(rows, 1 - my[core], 1), d), core) for rows, d, _ in jobs]
    kept = [outer(half(rows, my[core], 1), d) for rows, d, _ in jobs]

    dxt = jnp.dot(dk_b, w_key.T, preferred_element_type=jnp.float32) + jnp.dot(
        dv_b, w_value.T, preferred_element_type=jnp.float32
    )
    dxt = dxt.reshape(n_lang, cap, length, width)
    returned = [exchange(dxt[d], d) if d else dxt[d] for d in range(n_lang)]

    for step in range(len(jobs[0][2])):
        sent = []
        for j, (_, _, order) in enumerate(jobs):
            b = order[step]
            sent.append(swap(half(kept[j], 1 - my[b]) + half(got[j], 1 - my[b]), b))
        for j, (_, _, order) in enumerate(jobs):
            b = order[step]
            kept[j] = half(kept[j], my[b]) + half(got[j], my[b])
        got = sent
    factor = 1.0 / (sent_dev * n_lang * n_pair * length) ** 0.5
    whole = [((kept[j] + got[j]) * factor).astype(jnp.bfloat16) for j in range(3)]
    for step in reversed(range(-1, len(jobs[0][2]))):
        order = [core if step < 0 else job[2][step] for job in jobs]
        other = [swap(whole[j], order[j]) for j in range(3)]
        for j in range(3):
            first = my[order[j]] == 0
            whole[j] = jnp.concatenate([
                jnp.where(first, whole[j], other[j]), jnp.where(first, other[j], whole[j])], axis=0)

    grad_total = jnp.dot(dq_b, w_query.T, preferred_element_type=jnp.float32).reshape(
        sent_dev, length, width
    )
    owner = jnp.arange(sent_dev, dtype=jnp.int32)
    for d in range(n_lang):
        for c in range(cap):
            pick = (owner == listed[d][c])[:, None, None]
            grad_total = grad_total + jnp.where(pick, returned[d][c][None], 0.0)
    return (attended, grad_total.astype(jnp.bfloat16), whole[2], whole[1], whole[0])


def solution(mesh):
    in_specs = (
        P(("lang", "pair"), None, None),
        P(("lang", "pair"), None, None),
        P(),
        P(),
        P(),
        P(("lang", "pair"), None, None),
        P(("lang", "pair"), None),
        P(("lang", "pair"), None),
        P(("lang", "pair"), None),
    )
    out_specs = (P(("lang", "pair"), None, None), P(("lang", "pair"), None, None), P(), P(), P())
    return jax.shard_map(body, mesh=mesh, in_specs=in_specs, out_specs=out_specs, check_vma=False)
```

```python
import functools

import jax
import jax.numpy as jnp
from jax import lax
from jax.experimental import pallas as pl
from jax.experimental.pallas import tpu as pltpu
from jax.sharding import PartitionSpec as P

HEADS = 16
LANES = 128
GROUP = 256


def attend_kernel(
    src_ref, slot_ref, valid_ref, q_ref, k_ref, v_ref, g_ref,
    out_ref, dq_ref, dk_ref, dv_ref,
    bd, kv, kvt, out_t, dq_t, dkv, counts,
):
    n_src, length, width = q_ref.shape
    n_slot = k_ref.shape[0]
    size = LANES // 2
    scale = size ** (-0.5)
    blocks = width // LANES
    n_pairs = src_ref.shape[0]
    low = lax.broadcasted_iota(jnp.int32, (length, LANES), 1) < size

    def clear(i, _):
        counts[i] = 0
        return 0

    lax.fori_loop(0, n_src * n_slot, clear, 0)

    def count(j, _):
        key = src_ref[j] * n_slot + slot_ref[j]
        counts[key] = counts[key] + valid_ref[j]
        return 0

    lax.fori_loop(0, n_pairs, count, 0)

    def set_source(s, _):
        for b in range(blocks):
            cols = slice(b * LANES, (b + 1) * LANES)
            q = q_ref[s, :, cols].astype(jnp.float32) * scale
            g = pltpu.roll(g_ref[s, :, cols].astype(jnp.float32), size, 1)
            bd[s, 2 * b, :length] = jnp.where(low, q, 0.0).astype(jnp.bfloat16)
            bd[s, 2 * b, length:] = jnp.where(low, 0.0, g).astype(jnp.bfloat16)
            bd[s, 2 * b + 1, :length] = jnp.where(low, 0.0, q).astype(jnp.bfloat16)
            bd[s, 2 * b + 1, length:] = jnp.where(low, g, 0.0).astype(jnp.bfloat16)
        out_t[s] = jnp.zeros((width, length), jnp.float32)
        dq_t[s] = jnp.zeros((width, length), jnp.float32)
        return 0

    lax.fori_loop(0, n_src, set_source, 0)

    def set_slot(t, _):
        for b in range(blocks):
            cols = slice(b * LANES, (b + 1) * LANES)
            k = k_ref[t, :, cols].astype(jnp.float32)
            v = pltpu.roll(v_ref[t, :, cols].astype(jnp.float32), size, 1)
            even = jnp.where(low, k, v)
            odd = jnp.where(low, v, k)
            kv[t, 2 * b] = even.astype(jnp.bfloat16)
            kv[t, 2 * b + 1] = odd.astype(jnp.bfloat16)
            kvt[t, 2 * b] = even.T.astype(jnp.bfloat16)
            kvt[t, 2 * b + 1] = odd.T.astype(jnp.bfloat16)
            dkv[t, 2 * b] = jnp.zeros((length, LANES), jnp.float32)
            dkv[t, 2 * b + 1] = jnp.zeros((length, LANES), jnp.float32)
        return 0

    lax.fori_loop(0, n_slot, set_slot, 0)

    def combo(i, _):
        times = counts[i]

        @pl.when(times > 0)
        def _():
            s = i // n_slot
            t = i - s * n_slot
            w = times.astype(jnp.float32)
            both = []
            for h in range(2 * blocks):
                both.append(lax.dot_general(
                    kv[t, h], bd[s, h], (((1,), (1,)), ((), ())),
                    preferred_element_type=jnp.float32))
            mixed = []
            for h in range(2 * blocks):
                sc = both[h][:, :length]
                dp = both[h][:, length:]
                e = jnp.exp(sc - jnp.max(sc, axis=0, keepdims=True))
                p = e * (1.0 / jnp.sum(e, axis=0, keepdims=True))
                ds = p * (dp - jnp.sum(p * dp, axis=0, keepdims=True))
                mixed.append(jnp.concatenate(
                    [ds.astype(jnp.bfloat16), p.astype(jnp.bfloat16)], axis=1))
            for h in range(2 * blocks):
                x = mixed[h]
                dkv[t, h] += w * jnp.dot(x, bd[s, h], preferred_element_type=jnp.float32)
                r = jnp.dot(kvt[t, h], x, preferred_element_type=jnp.float32)
                rows = slice(h * size, (h + 1) * size)
                first, second = slice(0, size), slice(size, 2 * size)
                key_rows, value_rows = (first, second) if h % 2 == 0 else (second, first)
                dq_t[s, rows] += w * r[key_rows, :length]
                out_t[s, rows] += w * r[value_rows, length:]

        return 0

    lax.fori_loop(0, n_src * n_slot, combo, 0)

    def put_source(s, _):
        for b in range(blocks):
            cols = slice(b * LANES, (b + 1) * LANES)
            out_ref[s, :, cols] = out_t[s, cols].T.astype(jnp.bfloat16)
            dq_ref[s, :, cols] = (dq_t[s, cols].T * scale).astype(jnp.bfloat16)
        return 0

    lax.fori_loop(0, n_src, put_source, 0)

    def put_slot(t, _):
        for b in range(blocks):
            cols = slice(b * LANES, (b + 1) * LANES)
            even, odd = dkv[t, 2 * b], dkv[t, 2 * b + 1]
            dk_ref[t, :, cols] = jnp.where(low, even, odd).astype(jnp.bfloat16)
            dv_ref[t, :, cols] = pltpu.roll(jnp.where(low, odd, even), size, 1).astype(jnp.bfloat16)
        return 0

    lax.fori_loop(0, n_slot, put_slot, 0)


def attend(src, slot, valid, queries, keys, values, cotangent):
    n_src, length, width = queries.shape
    n_slot = keys.shape[0]
    heads = 2 * GROUP // LANES
    smem = pl.BlockSpec(memory_space=pltpu.SMEM)

    def cut(rows):
        return pl.BlockSpec((rows, length, GROUP), lambda i: (0, 0, i))

    def made(rows):
        return jax.ShapeDtypeStruct((rows, length, width), jnp.bfloat16)

    return pl.pallas_call(
        attend_kernel,
        grid=(width // GROUP,),
        in_specs=[smem, smem, smem, cut(n_src), cut(n_slot), cut(n_slot), cut(n_src)],
        out_specs=[cut(n_src), cut(n_src), cut(n_slot), cut(n_slot)],
        out_shape=[made(n_src), made(n_src), made(n_slot), made(n_slot)],
        scratch_shapes=[
            pltpu.VMEM((n_src, heads, 2 * length, LANES), jnp.bfloat16),
            pltpu.VMEM((n_slot, heads, length, LANES), jnp.bfloat16),
            pltpu.VMEM((n_slot, heads, LANES, length), jnp.bfloat16),
            pltpu.VMEM((n_src, GROUP, length), jnp.float32),
            pltpu.VMEM((n_src, GROUP, length), jnp.float32),
            pltpu.VMEM((n_slot, heads, length, LANES), jnp.float32),
            pltpu.SMEM((n_src * n_slot,), jnp.int32),
        ],
        compiler_params=pltpu.CompilerParams(vmem_limit_bytes=32 * 1024 * 1024),
        cost_estimate=pl.CostEstimate(
            flops=12000000000, bytes_accessed=30000000, transcendentals=4000000),
    )(src, slot, valid, queries, keys, values, cotangent)


def project(rows, weight):
    return (
        jnp.dot(rows.reshape(-1, rows.shape[-1]), weight, preferred_element_type=jnp.float32)
        .astype(jnp.bfloat16)
        .reshape(rows.shape)
    )


AXES = ("lang", "pair")


def swap(x, bit):
    n = lax.axis_size("lang") * lax.axis_size("pair")
    return lax.ppermute(x, AXES, [(i, i ^ (1 << bit)) for i in range(n)])


def half(x, which, axis=0):
    rows = x.shape[axis] // 2
    return lax.dynamic_slice_in_dim(x, which * rows, rows, axis)


def flip(x, d):
    b = 0
    out = x
    while (1 << b) <= d:
        if (d >> b) & 1:
            out = out + (1 - 2 * ((x // (1 << b)) % 2)) * (1 << b)
        b += 1
    return out


def reduce_kernel(
    n_lang, n_pair, orders, factor,
    kept0, kept1, kept2, got0, got1, got2, dxt,
    whole0, whole1, whole2, ret,
    kbuf, rbuf, sbuf,
    rs_send, rs_recv, ag_send, ag_recv, fw_send, fw_recv, ret_send, ret_recv,
):
    lang, pair = lax.axis_index("lang"), lax.axis_index("pair")
    pair_bits = n_pair.bit_length() - 1
    mesh_id = pl.DeviceIdType.MESH
    kept, got, whole = (kept0, kept1, kept2), (got0, got1, got2), (whole0, whole1, whole2)
    height, cols = kept0.shape
    steps = len(orders[0])

    def across(b):
        if b < pair_bits:
            return (lang, flip(pair, 1 << b))
        return (flip(lang, 1 << (b - pair_bits)), pair)

    def mine(b):
        if b < pair_bits:
            return (pair // (1 << b)) % 2
        return (lang // (1 << (b - pair_bits))) % 2

    core = pair_bits
    col = pl.multiple_of(mine(core) * cols, cols)

    partners = [across(b) for b in range(pair_bits)] + [
        (flip(lang, d), pair) for d in range(1, n_lang)]
    barrier = pltpu.get_barrier_semaphore()
    for p in partners:
        pl.semaphore_signal(barrier, inc=1, device_id=p, device_id_type=mesh_id)
    pl.semaphore_wait(barrier, len(partners))

    started = []

    def send(src, dst, send_sem, recv_sem, device):
        copy = pltpu.make_async_remote_copy(
            src_ref=src, dst_ref=dst, send_sem=send_sem, recv_sem=recv_sem,
            device_id=device, device_id_type=mesh_id)
        copy.start()
        started.append(copy)
        return copy

    pending = [None, None, None]
    for step in range(steps):
        rows = height >> (step + 1)
        at = pl.ds(height - (height >> step), rows)
        before = height - 2 * (height >> step)
        for j in range(3):
            b = orders[j][step]
            if step:
                pending[j].wait_recv()

            def both(which):
                if step == 0:
                    part = pl.ds(pl.multiple_of(which * rows, rows), rows)
                    return kept[j][part] + got[j][part]
                part = pl.ds(pl.multiple_of(before + which * rows, rows), rows)
                return kbuf[j, part] + rbuf[j, part]

            sbuf[j, at] = both(1 - mine(b))
            pending[j] = send(sbuf.at[j, at], rbuf.at[j, at], rs_send.at[j, step],
                              rs_recv.at[j, step], across(b))
            kbuf[j, at] = both(mine(b))
        if step == 0:
            returns = [
                send(dxt.at[d], ret.at[d - 1], ret_send.at[d - 1], ret_recv.at[d - 1],
                     (flip(lang, d), pair))
                for d in range(1, n_lang)]

    arrived = []

    def forward(j, n, row, rows):
        part = whole[j].at[pl.ds(row, rows), pl.ds(col, cols)]
        arrived.append(send(part, part, fw_send.at[j, n], fw_recv.at[j, n], across(core)))

    offsets = []
    for j in range(3):
        row, offs = 0, []
        for step in range(steps):
            rows = height >> (step + 1)
            row = row + mine(orders[j][step]) * rows
            offs.append(row)
        offsets.append(offs)

    last = height >> steps
    for step in reversed(range(steps)):
        rows = height >> (step + 1)
        for j in range(3):
            b = orders[j][step]
            row = pl.multiple_of(offsets[j][step], rows)
            pending[j].wait_recv()
            if step == steps - 1:
                at = pl.ds(height - (height >> step), last)
                total = kbuf[j, at] + rbuf[j, at]
                whole[j][pl.ds(row, last), pl.ds(col, cols)] = (total * factor).astype(jnp.bfloat16)
            part = whole[j].at[pl.ds(row, rows), pl.ds(col, cols)]
            pending[j] = send(part, part, ag_send.at[j, step], ag_recv.at[j, step], across(b))
            if step == steps - 1:
                forward(j, steps, row, rows)
            else:
                up = orders[j][step + 1]
                small = height >> (step + 2)
                other = offsets[j][step + 1] + (1 - 2 * mine(up)) * small
                forward(j, step + 1, pl.multiple_of(other, small), small)
    for j in range(3):
        pending[j].wait_recv()
        b, rows = orders[j][0], height >> 1
        forward(j, 0, pl.multiple_of((1 - mine(b)) * rows, rows), rows)
    for copy in returns + arrived:
        copy.wait_recv()
    for copy in started:
        copy.wait_send()


def reduce_all(n_lang, n_pair, orders, factor, kept, got, dxt):
    height, cols = kept[0].shape
    steps = len(orders[0])
    vmem = pl.BlockSpec(memory_space=pltpu.VMEM)
    sem = pltpu.SemaphoreType.DMA
    made = jax.ShapeDtypeStruct((height, 2 * cols), jnp.bfloat16)
    return pl.pallas_call(
        functools.partial(reduce_kernel, n_lang, n_pair, orders, factor),
        in_specs=[vmem] * 7,
        out_specs=[vmem] * 4,
        out_shape=[made, made, made,
                   jax.ShapeDtypeStruct((n_lang - 1,) + dxt.shape[1:], dxt.dtype)],
        scratch_shapes=[pltpu.VMEM((3, height, cols), jnp.float32)] * 3 + [
            sem((3, steps)), sem((3, steps)), sem((3, steps)), sem((3, steps)),
            sem((3, steps + 1)), sem((3, steps + 1)), sem((n_lang - 1,)), sem((n_lang - 1,))],
        compiler_params=pltpu.CompilerParams(
            collective_id=0, has_side_effects=True, vmem_limit_bytes=50 * 1024 * 1024),
    )(*kept, *got, dxt)


def body(sentences, cotangent, w_query, w_key, w_value, send_rows, pair_src, pair_slot, pair_valid):
    sent_dev, length, width = sentences.shape
    n_lang = lax.axis_size("lang")
    n_pair = lax.axis_size("pair")
    cap = send_rows.shape[2]
    slots = n_lang * cap
    lang = lax.axis_index("lang")
    me = lang * n_pair + lax.axis_index("pair")
    pair_bits = n_pair.bit_length() - 1
    lang_bits = n_lang.bit_length() - 1
    core = pair_bits
    low = list(range(pair_bits // 2))
    high = list(range(pair_bits // 2, pair_bits))
    upper = list(range(pair_bits + 1, pair_bits + lang_bits))

    def exchange(x, d):
        return lax.ppermute(x, "lang", [(i, i ^ d) for i in range(n_lang)])

    listed = [lax.dynamic_index_in_dim(send_rows[0], lang ^ d, 0, False) for d in range(n_lang)]
    received = []
    for d in range(n_lang):
        block = jnp.take(sentences, listed[d], axis=0)
        received.append(exchange(block, d) if d else block)
    received = jnp.concatenate(received, axis=0)
    slot = pair_slot[0]
    slot = ((slot // cap) ^ lang) * cap + slot % cap

    queries = project(sentences, w_query)
    keys = project(received, w_key)
    values = project(received, w_value)
    attended, dq, dk, dv = attend(
        pair_src[0], slot, pair_valid[0], queries, keys, values, cotangent)
    flat = (-1, width)
    dq_b, dk_b, dv_b = dq.reshape(flat), dk.reshape(flat), dv.reshape(flat)

    my = {b: (me >> b) & 1 for b in range(pair_bits + lang_bits)}
    own_flat = sentences.reshape(flat)
    recv_flat = received.reshape(flat)
    contract = (((0,), (0,)), ((), ()))

    def outer(rows, d):
        return lax.dot_general(rows, d, contract, preferred_element_type=jnp.float32)

    jobs = [
        (recv_flat, dv_b, high + low + upper),
        (recv_flat, dk_b, upper + high + low),
        (own_flat, dq_b, low + upper + high),
    ]
    got = [swap(outer(rows, half(d, 1 - my[core], 1)), core) for rows, d, _ in jobs]
    kept = [outer(rows, half(d, my[core], 1)) for rows, d, _ in jobs]
    dxt = jnp.dot(dk_b, w_key.T, preferred_element_type=jnp.float32) + jnp.dot(
        dv_b, w_value.T, preferred_element_type=jnp.float32
    )
    dxt = dxt.reshape(n_lang, cap, length, width)
    factor = 1.0 / (sent_dev * n_lang * n_pair * length) ** 0.5
    grad_wv, grad_wk, grad_wq, ret = reduce_all(
        n_lang, n_pair, [order for _, _, order in jobs], factor, kept, got, dxt)
    returned = [dxt[0]] + [ret[d] for d in range(n_lang - 1)]

    grad_total = jnp.dot(dq_b, w_query.T, preferred_element_type=jnp.float32).reshape(
        sent_dev, length, width
    )
    owner = jnp.arange(sent_dev, dtype=jnp.int32)
    for d in range(n_lang):
        for c in range(cap):
            pick = (owner == listed[d][c])[:, None, None]
            grad_total = grad_total + jnp.where(pick, returned[d][c][None], 0.0)
    return (attended, grad_total.astype(jnp.bfloat16), grad_wq, grad_wk, grad_wv)


def solution(mesh):
    in_specs = (
        P(("lang", "pair"), None, None),
        P(("lang", "pair"), None, None),
        P(),
        P(),
        P(),
        P(("lang", "pair"), None, None),
        P(("lang", "pair"), None),
        P(("lang", "pair"), None),
        P(("lang", "pair"), None),
    )
    out_specs = (P(("lang", "pair"), None, None), P(("lang", "pair"), None, None), P(), P(), P())
    return jax.shard_map(body, mesh=mesh, in_specs=in_specs, out_specs=out_specs, check_vma=False)
```

```python
import functools

import jax
import jax.numpy as jnp
from jax import lax
from jax.experimental import pallas as pl
from jax.experimental.pallas import tpu as pltpu
from jax.sharding import PartitionSpec as P

HEADS = 16
LANES = 128
GROUP = 256


def attend_kernel(
    src_ref, slot_ref, valid_ref, q_ref, k_ref, v_ref, g_ref,
    out_ref, dq_ref, dk_ref, dv_ref,
    bd, kv, kvt, out_t, dq_t, dkv, counts,
):
    n_src, length, width = q_ref.shape
    n_slot = k_ref.shape[0]
    size = LANES // 2
    scale = size ** (-0.5)
    blocks = width // LANES
    n_pairs = src_ref.shape[0]
    low = lax.broadcasted_iota(jnp.int32, (length, LANES), 1) < size

    def clear(i, _):
        counts[i] = 0
        return 0

    lax.fori_loop(0, n_src * n_slot, clear, 0)

    def count(j, _):
        key = src_ref[j] * n_slot + slot_ref[j]
        counts[key] = counts[key] + valid_ref[j]
        return 0

    lax.fori_loop(0, n_pairs, count, 0)

    def set_source(s, _):
        for b in range(blocks):
            cols = slice(b * LANES, (b + 1) * LANES)
            q = q_ref[s, :, cols].astype(jnp.float32) * scale
            g = pltpu.roll(g_ref[s, :, cols].astype(jnp.float32), size, 1)
            bd[s, 2 * b, :length] = jnp.where(low, q, 0.0).astype(jnp.bfloat16)
            bd[s, 2 * b, length:] = jnp.where(low, 0.0, g).astype(jnp.bfloat16)
            bd[s, 2 * b + 1, :length] = jnp.where(low, 0.0, q).astype(jnp.bfloat16)
            bd[s, 2 * b + 1, length:] = jnp.where(low, g, 0.0).astype(jnp.bfloat16)
        out_t[s] = jnp.zeros((width, length), jnp.float32)
        dq_t[s] = jnp.zeros((width, length), jnp.float32)
        return 0

    lax.fori_loop(0, n_src, set_source, 0)

    def set_slot(t, _):
        for b in range(blocks):
            cols = slice(b * LANES, (b + 1) * LANES)
            k = k_ref[t, :, cols].astype(jnp.float32)
            v = pltpu.roll(v_ref[t, :, cols].astype(jnp.float32), size, 1)
            even = jnp.where(low, k, v)
            odd = jnp.where(low, v, k)
            kv[t, 2 * b] = even.astype(jnp.bfloat16)
            kv[t, 2 * b + 1] = odd.astype(jnp.bfloat16)
            kvt[t, 2 * b] = even.T.astype(jnp.bfloat16)
            kvt[t, 2 * b + 1] = odd.T.astype(jnp.bfloat16)
            dkv[t, 2 * b] = jnp.zeros((length, LANES), jnp.float32)
            dkv[t, 2 * b + 1] = jnp.zeros((length, LANES), jnp.float32)
        return 0

    lax.fori_loop(0, n_slot, set_slot, 0)

    def combo(i, _):
        times = counts[i]

        @pl.when(times > 0)
        def _():
            s = i // n_slot
            t = i - s * n_slot
            w = times.astype(jnp.float32)
            both = []
            for h in range(2 * blocks):
                both.append(lax.dot_general(
                    kv[t, h], bd[s, h], (((1,), (1,)), ((), ())),
                    preferred_element_type=jnp.float32))
            mixed = []
            for h in range(2 * blocks):
                sc = both[h][:, :length]
                dp = both[h][:, length:]
                e = jnp.exp(sc - jnp.max(sc, axis=0, keepdims=True))
                p = e * (1.0 / jnp.sum(e, axis=0, keepdims=True))
                ds = p * (dp - jnp.sum(p * dp, axis=0, keepdims=True))
                mixed.append(jnp.concatenate(
                    [ds.astype(jnp.bfloat16), p.astype(jnp.bfloat16)], axis=1))
            for h in range(2 * blocks):
                x = mixed[h]
                dkv[t, h] += w * jnp.dot(x, bd[s, h], preferred_element_type=jnp.float32)
                r = jnp.dot(kvt[t, h], x, preferred_element_type=jnp.float32)
                rows = slice(h * size, (h + 1) * size)
                first, second = slice(0, size), slice(size, 2 * size)
                key_rows, value_rows = (first, second) if h % 2 == 0 else (second, first)
                dq_t[s, rows] += w * r[key_rows, :length]
                out_t[s, rows] += w * r[value_rows, length:]

        return 0

    lax.fori_loop(0, n_src * n_slot, combo, 0)

    def put_source(s, _):
        for b in range(blocks):
            cols = slice(b * LANES, (b + 1) * LANES)
            out_ref[s, :, cols] = out_t[s, cols].T.astype(jnp.bfloat16)
            dq_ref[s, :, cols] = (dq_t[s, cols].T * scale).astype(jnp.bfloat16)
        return 0

    lax.fori_loop(0, n_src, put_source, 0)

    def put_slot(t, _):
        for b in range(blocks):
            cols = slice(b * LANES, (b + 1) * LANES)
            even, odd = dkv[t, 2 * b], dkv[t, 2 * b + 1]
            dk_ref[t, :, cols] = jnp.where(low, even, odd).astype(jnp.bfloat16)
            dv_ref[t, :, cols] = pltpu.roll(jnp.where(low, odd, even), size, 1).astype(jnp.bfloat16)
        return 0

    lax.fori_loop(0, n_slot, put_slot, 0)


def attend(src, slot, valid, queries, keys, values, cotangent):
    n_src, length, width = queries.shape
    n_slot = keys.shape[0]
    heads = 2 * GROUP // LANES
    smem = pl.BlockSpec(memory_space=pltpu.SMEM)

    def cut(rows):
        return pl.BlockSpec((rows, length, GROUP), lambda i: (0, 0, i))

    def made(rows):
        return jax.ShapeDtypeStruct((rows, length, width), jnp.bfloat16)

    return pl.pallas_call(
        attend_kernel,
        grid=(width // GROUP,),
        in_specs=[smem, smem, smem, cut(n_src), cut(n_slot), cut(n_slot), cut(n_src)],
        out_specs=[cut(n_src), cut(n_src), cut(n_slot), cut(n_slot)],
        out_shape=[made(n_src), made(n_src), made(n_slot), made(n_slot)],
        scratch_shapes=[
            pltpu.VMEM((n_src, heads, 2 * length, LANES), jnp.bfloat16),
            pltpu.VMEM((n_slot, heads, length, LANES), jnp.bfloat16),
            pltpu.VMEM((n_slot, heads, LANES, length), jnp.bfloat16),
            pltpu.VMEM((n_src, GROUP, length), jnp.float32),
            pltpu.VMEM((n_src, GROUP, length), jnp.float32),
            pltpu.VMEM((n_slot, heads, length, LANES), jnp.float32),
            pltpu.SMEM((n_src * n_slot,), jnp.int32),
        ],
        compiler_params=pltpu.CompilerParams(vmem_limit_bytes=32 * 1024 * 1024),
        cost_estimate=pl.CostEstimate(
            flops=12000000000, bytes_accessed=30000000, transcendentals=4000000),
    )(src, slot, valid, queries, keys, values, cotangent)


def project(rows, weight):
    return (
        jnp.dot(rows.reshape(-1, rows.shape[-1]), weight, preferred_element_type=jnp.float32)
        .astype(jnp.bfloat16)
        .reshape(rows.shape)
    )


AXES = ("lang", "pair")


def swap(x, bit):
    n = lax.axis_size("lang") * lax.axis_size("pair")
    return lax.ppermute(x, AXES, [(i, i ^ (1 << bit)) for i in range(n)])


def half(x, which, axis=0):
    rows = x.shape[axis] // 2
    return lax.dynamic_slice_in_dim(x, which * rows, rows, axis)


def flip(x, d):
    b = 0
    out = x
    while (1 << b) <= d:
        if (d >> b) & 1:
            out = out + (1 - 2 * ((x // (1 << b)) % 2)) * (1 << b)
        b += 1
    return out


def reduce_kernel(
    n_lang, n_pair, orders, factor,
    kept0, kept1, kept2, got0, got1, got2, dxt,
    whole0, whole1, whole2, ret,
    kbuf, rbuf, sbuf, sbuf_b, rbuf_b,
    rs_send, rs_recv, ag_send, ag_recv, fw_send, fw_recv, ret_send, ret_recv,
):
    lang, pair = lax.axis_index("lang"), lax.axis_index("pair")
    pair_bits = n_pair.bit_length() - 1
    mesh_id = pl.DeviceIdType.MESH
    kept, got, whole = (kept0, kept1, kept2), (got0, got1, got2), (whole0, whole1, whole2)
    height, job_cols = kept0.shape
    n = len(orders)
    per = n // 3
    cols = job_cols // per
    steps = len(orders[0])

    def across(b):
        if b < pair_bits:
            return (lang, flip(pair, 1 << b))
        return (flip(lang, 1 << (b - pair_bits)), pair)

    def mine(b):
        if b < pair_bits:
            return (pair // (1 << b)) % 2
        return (lang // (1 << (b - pair_bits))) % 2

    core = pair_bits
    col = [pl.multiple_of(mine(core) * job_cols + (j % per) * cols, cols) for j in range(n)]
    sub = [slice((j % per) * cols, (j % per + 1) * cols) for j in range(n)]

    partners = [across(b) for b in range(pair_bits)] + [
        (flip(lang, d), pair) for d in range(1, n_lang)]
    barrier = pltpu.get_barrier_semaphore()
    for p in partners:
        pl.semaphore_signal(barrier, inc=1, device_id=p, device_id_type=mesh_id)
    pl.semaphore_wait(barrier, len(partners))

    started = []

    def send(src, dst, send_sem, recv_sem, device):
        copy = pltpu.make_async_remote_copy(
            src_ref=src, dst_ref=dst, send_sem=send_sem, recv_sem=recv_sem,
            device_id=device, device_id_type=mesh_id)
        copy.start()
        started.append(copy)
        return copy

    pending = [None] * n
    for step in range(steps):
        rows = height >> (step + 1)
        at = pl.ds(height - (height >> step), rows)
        before = height - 2 * (height >> step)
        for j in range(n):
            b = orders[j][step]
            if step:
                pending[j].wait_recv()

            def both(which):
                if step == 0:
                    part = pl.ds(pl.multiple_of(which * rows, rows), rows)
                    return kept[j // per][part, sub[j]] + got[j // per][part, sub[j]]
                part = pl.ds(pl.multiple_of(before + which * rows, rows), rows)
                if step == 1:
                    here = pl.ds(pl.multiple_of(which * rows, rows), rows)
                    return kbuf[j, part] + rbuf_b[j, here].astype(jnp.float32)
                return kbuf[j, part] + rbuf[j, part]

            if step == 0:
                sbuf_b[j] = both(1 - mine(b)).astype(jnp.bfloat16)
                source, target = sbuf_b.at[j], rbuf_b.at[j]
            else:
                sbuf[j, at] = both(1 - mine(b))
                source, target = sbuf.at[j, at], rbuf.at[j, at]
            pending[j] = send(source, target, rs_send.at[j, step], rs_recv.at[j, step], across(b))
            kbuf[j, at] = both(mine(b))
        if step == 1:
            returns = [
                send(dxt.at[d], ret.at[d - 1], ret_send.at[d - 1], ret_recv.at[d - 1],
                     (flip(lang, d), pair))
                for d in range(1, n_lang)]

    arrived = []

    def forward(j, at, row, rows):
        part = whole[j // per].at[pl.ds(row, rows), pl.ds(col[j], cols)]
        arrived.append(send(part, part, fw_send.at[j, at], fw_recv.at[j, at], across(core)))

    offsets = []
    for j in range(n):
        row, offs = 0, []
        for step in range(steps):
            rows = height >> (step + 1)
            row = row + mine(orders[j][step]) * rows
            offs.append(row)
        offsets.append(offs)

    last = height >> steps
    for step in reversed(range(steps)):
        rows = height >> (step + 1)
        for j in range(n):
            b = orders[j][step]
            row = pl.multiple_of(offsets[j][step], rows)
            pending[j].wait_recv()
            if step == steps - 1:
                at = pl.ds(height - (height >> step), last)
                total = kbuf[j, at] + rbuf[j, at]
                whole[j // per][pl.ds(row, last), pl.ds(col[j], cols)] = (
                    total * factor).astype(jnp.bfloat16)
            part = whole[j // per].at[pl.ds(row, rows), pl.ds(col[j], cols)]
            pending[j] = send(part, part, ag_send.at[j, step], ag_recv.at[j, step], across(b))
            if step == steps - 1:
                forward(j, steps, row, rows)
            else:
                up = orders[j][step + 1]
                small = height >> (step + 2)
                other = offsets[j][step + 1] + (1 - 2 * mine(up)) * small
                forward(j, step + 1, pl.multiple_of(other, small), small)
    for j in range(n):
        pending[j].wait_recv()
        b, rows = orders[j][0], height >> 1
        forward(j, 0, pl.multiple_of((1 - mine(b)) * rows, rows), rows)
    for copy in returns + arrived:
        copy.wait_recv()
    for copy in started:
        copy.wait_send()


def reduce_all(n_lang, n_pair, orders, factor, kept, got, dxt):
    height, cols = kept[0].shape
    steps, n = len(orders[0]), len(orders)
    vmem = pl.BlockSpec(memory_space=pltpu.VMEM)
    sem = pltpu.SemaphoreType.DMA
    made = jax.ShapeDtypeStruct((height, 2 * cols), jnp.bfloat16)
    return pl.pallas_call(
        functools.partial(reduce_kernel, n_lang, n_pair, orders, factor),
        in_specs=[vmem] * 7,
        out_specs=[vmem] * 4,
        out_shape=[made, made, made,
                   jax.ShapeDtypeStruct((n_lang - 1,) + dxt.shape[1:], dxt.dtype)],
        scratch_shapes=[pltpu.VMEM((n, height, 3 * cols // n), jnp.float32)] * 3 + [
            pltpu.VMEM((n, height // 2, 3 * cols // n), jnp.bfloat16)] * 2 + [
            sem((n, steps)), sem((n, steps)), sem((n, steps)), sem((n, steps)),
            sem((n, steps + 1)), sem((n, steps + 1)), sem((n_lang - 1,)), sem((n_lang - 1,))],
        compiler_params=pltpu.CompilerParams(
            collective_id=0, has_side_effects=True, vmem_limit_bytes=50 * 1024 * 1024),
    )(*kept, *got, dxt)


def body(sentences, cotangent, w_query, w_key, w_value, send_rows, pair_src, pair_slot, pair_valid):
    sent_dev, length, width = sentences.shape
    n_lang = lax.axis_size("lang")
    n_pair = lax.axis_size("pair")
    cap = send_rows.shape[2]
    slots = n_lang * cap
    lang = lax.axis_index("lang")
    me = lang * n_pair + lax.axis_index("pair")
    pair_bits = n_pair.bit_length() - 1
    lang_bits = n_lang.bit_length() - 1
    core = pair_bits
    low = list(range(pair_bits // 2))
    high = list(range(pair_bits // 2, pair_bits))
    upper = list(range(pair_bits + 1, pair_bits + lang_bits))

    def exchange(x, d):
        return lax.ppermute(x, "lang", [(i, i ^ d) for i in range(n_lang)])

    listed = [lax.dynamic_index_in_dim(send_rows[0], lang ^ d, 0, False) for d in range(n_lang)]
    received = []
    for d in range(n_lang):
        block = jnp.take(sentences, listed[d], axis=0)
        received.append(exchange(block, d) if d else block)
    received = jnp.concatenate(received, axis=0)
    slot = pair_slot[0]
    slot = ((slot // cap) ^ lang) * cap + slot % cap

    queries = project(sentences, w_query)
    keys = project(received, w_key)
    values = project(received, w_value)
    attended, dq, dk, dv = attend(
        pair_src[0], slot, pair_valid[0], queries, keys, values, cotangent)
    flat = (-1, width)
    dq_b, dk_b, dv_b = dq.reshape(flat), dk.reshape(flat), dv.reshape(flat)

    my = {b: (me >> b) & 1 for b in range(pair_bits + lang_bits)}
    own_flat = sentences.reshape(flat)
    recv_flat = received.reshape(flat)
    contract = (((0,), (0,)), ((), ()))

    def outer(rows, d):
        return lax.dot_general(rows, d, contract, preferred_element_type=jnp.float32)

    jobs = [(recv_flat, dv_b), (recv_flat, dk_b), (own_flat, dq_b)]
    orders = [
        high + low + upper, high + upper + low,
        upper + high + low, upper + low + high,
        low + upper + high, low + high + upper,
    ]
    got = [swap(outer(rows, half(d, 1 - my[core], 1)), core) for rows, d in jobs]
    kept = [outer(rows, half(d, my[core], 1)) for rows, d in jobs]
    dxt = jnp.dot(dk_b, w_key.T, preferred_element_type=jnp.float32) + jnp.dot(
        dv_b, w_value.T, preferred_element_type=jnp.float32
    )
    dxt = dxt.reshape(n_lang, cap, length, width)
    factor = 1.0 / (sent_dev * n_lang * n_pair * length) ** 0.5
    grad_wv, grad_wk, grad_wq, ret = reduce_all(
        n_lang, n_pair, orders, factor, kept, got, dxt)
    returned = [dxt[0]] + [ret[d] for d in range(n_lang - 1)]

    grad_total = jnp.dot(dq_b, w_query.T, preferred_element_type=jnp.float32).reshape(
        sent_dev, length, width
    )
    owner = jnp.arange(sent_dev, dtype=jnp.int32)
    for d in range(n_lang):
        for c in range(cap):
            pick = (owner == listed[d][c])[:, None, None]
            grad_total = grad_total + jnp.where(pick, returned[d][c][None], 0.0)
    return (attended, grad_total.astype(jnp.bfloat16), grad_wq, grad_wk, grad_wv)


def solution(mesh):
    in_specs = (
        P(("lang", "pair"), None, None),
        P(("lang", "pair"), None, None),
        P(),
        P(),
        P(),
        P(("lang", "pair"), None, None),
        P(("lang", "pair"), None),
        P(("lang", "pair"), None),
        P(("lang", "pair"), None),
    )
    out_specs = (P(("lang", "pair"), None, None), P(("lang", "pair"), None, None), P(), P(), P())
    return jax.shard_map(body, mesh=mesh, in_specs=in_specs, out_specs=out_specs, check_vma=False)
```
